32 devices in a mesh: store: 8 (over z, x), tensor: 4 (over y, core).
Axes of the slice: x: 2, y: 2, z: 4, core: 2. Of those that a mesh axis runs over, the one named last changes fastest.
Arguments:
- hidden: bfloat16 [8192, 12288], P('store', 'tensor'), may hold values from -6 to 6
- kv_weight: bfloat16 [12288, 2048], P('tensor', 'store'), may hold values from -0.0546875 to 0.0546875
- pages: bfloat16 [256, 128, 2048], P('store', None, 'tensor'), may hold values from -8 to 8
- queries: bfloat16 [8192, 6144], P('store', 'tensor'), may hold values from -8 to 8
- page_owner: int32 [16, 16], replicated, may hold values from 0 to 7, as said below
- page_slot: int32 [16, 16], replicated, may hold values from 0 to 31
- span_order: int32 [16, 16], P('store'), may hold values from 0 to 15, each once within a row
- positions: int32 [16, 16, 32], P('store'), may hold values from 2 to 127, as said below
- counts: int32 [16, 16], P('store'), may hold values from 1 to 32, as said below
Outputs:
- attended: bfloat16 [8192, 6144], P('store', 'tensor')
- new_kv: bfloat16 [8192, 2048], P('store', 'tensor')
The draws below stay inside these ranges and needn't reach their ends.
Inputs may be any that keep to these rules, and one draw needn't show every extreme that they name: `page_owner`: request r is served at store index r // 2. Among the 32 pages of the requests served at one store index, each owner holds at most 8, and some owner exactly 8. `positions`: each row increases strictly. `counts`: every request has a span with 32.
All inputs are finite; a program needn't handle non-finite values.
Results may differ from the reference program's by a relative error of at most 0.0053.
Values may be sent and summed in bfloat16 or wider, within the bound.
A program may use at most 128 MiB of HBM per device.

```python
import math
import jax
import jax.numpy as jnp
from jax import lax

D = 12288
HEAD = 128
KVH = 8
QH = 48
SPAN = 128
SPANS = 16
RB = 32
REQ_DEV = 2
REQUESTS = 16
CAP = 8
SLOTS = 32
ROWS = 8192
N_STORE = 8


def page_table(key):
    entries = REQ_DEV * SPANS
    capacity_all = N_STORE * CAP
    group_keys = jax.random.split(jax.random.fold_in(key, 21), N_STORE)

    def one_group(group_key):
        first_key, second_key = jax.random.split(group_key)
        shuffled = jax.random.permutation(first_key, capacity_all)
        chosen = shuffled[0] // CAP
        ranking = jnp.where(shuffled // CAP == chosen, shuffled % CAP, CAP + jnp.arange(capacity_all))
        picked = shuffled[jnp.argsort(ranking)][:entries] // CAP
        return jax.random.permutation(second_key, picked)
    owners = jax.vmap(one_group)(group_keys).reshape(REQUESTS, SPANS).astype(jnp.int32)
    slot_table = jax.random.randint(jax.random.fold_in(key, 22), (REQUESTS, SPANS), 0, SLOTS).astype(jnp.int32)
    return (owners, slot_table)


def draw_page_owner(key, part):
    return page_table(key)[0]


def draw_page_slot(key, part):
    return page_table(key)[1]


def draw_pages(key, part):
    key = jax.random.fold_in(key, 31)
    base = jnp.clip(jax.random.normal(key, (N_STORE * SLOTS, SPAN, KVH * 2 * HEAD), jnp.float32), -8.0, 8.0)
    return base.astype(jnp.bfloat16)


def draw_queries(key, part):
    key = jax.random.fold_in(key, 41)
    base = jnp.clip(jax.random.normal(key, (ROWS, QH * HEAD), jnp.float32), -8.0, 8.0)
    return base.astype(jnp.bfloat16)


def draw_positions(key, part):
    key = jax.random.fold_in(key, 51)
    row_keys = jax.random.split(key, REQUESTS * SPANS)

    def one_row(row_key):
        return jnp.sort(jax.random.permutation(row_key, SPAN - 2)[:RB]) + 2
    return jax.vmap(one_row)(row_keys).reshape(REQUESTS, SPANS, RB).astype(jnp.int32)


def draw_counts(key, part):
    key = jax.random.fold_in(key, 61)
    drawn = jax.random.randint(jax.random.fold_in(key, 1), (REQUESTS, SPANS), 1, RB + 1)
    full_at = jax.random.randint(jax.random.fold_in(key, 2), (REQUESTS, 1), 0, SPANS)
    return jnp.where(jnp.arange(SPANS)[None, :] == full_at, RB, drawn).astype(jnp.int32)


def block_scale(own_key, shape, cuts, low, high):
    gain = 1.0
    for dim, parts in cuts:
        heights = jax.random.uniform(jax.random.fold_in(jax.random.fold_in(own_key, 6), dim), (parts,), jnp.float32, low / len(cuts), high / len(cuts))
        gain = gain * jnp.repeat(jnp.exp(heights), shape[dim] // parts).reshape((-1,) + (1,) * (len(shape) - 1 - dim))
    return gain


def scatter_about(rng, dims, spread, bound, shards=(), kind=jnp.bfloat16):
    level = block_scale(rng, dims, shards, -0.22, 0.18) if shards else 1.0
    values = jax.random.normal(rng, dims, jnp.float32) * spread * level
    return jnp.minimum(jnp.maximum(values, -bound), bound).astype(kind)


def setup_inputs(seed: int = 0) -> dict:
    keys = jax.random.split(jax.random.key(seed), 10)
    return {
        "hidden": scatter_about(keys[0], (ROWS, D), 1.0, 6.0, ((0, 8), (1, 4))),
        "kv_weight": scatter_about(keys[1], (D, KVH * 2 * HEAD), D ** -0.5, 0.0546875, ((0, 4), (1, 8))),
        "pages": draw_pages(jax.random.fold_in(keys[9], 71), 0),
        "queries": draw_queries(jax.random.fold_in(keys[9], 71), 0),
        "page_owner": draw_page_owner(jax.random.fold_in(keys[9], 71), 0),
        "page_slot": draw_page_slot(jax.random.fold_in(keys[9], 71), 0),
        "span_order": jax.vmap(lambda own: jax.random.permutation(own, SPANS))(jax.random.split(keys[6], REQUESTS)).reshape((REQUESTS, SPANS)).astype(jnp.int32),
        "positions": draw_positions(jax.random.fold_in(keys[9], 71), 0),
        "counts": draw_counts(jax.random.fold_in(keys[9], 71), 0),
    }


def blend_attend(request_queries, fresh_rows, cached, span_rank, recompute_pos, row_used):
    spans, span_len, kv_width = cached.shape
    per_span = recompute_pos.shape[1]
    kv_heads = kv_width // (2 * HEAD)
    head_group = request_queries.shape[1] // (kv_heads * HEAD)
    marked = (recompute_pos[:, :, None] == jnp.arange(span_len)[None, None, :]) & row_used[:, :, None]
    placed = jnp.einsum('cjt,cjw->ctw', marked.astype(jnp.float32), fresh_rows.reshape(spans, per_span, kv_width).astype(jnp.float32))
    replaced = jnp.any(marked, axis=1)[:, :, None]
    blended = jnp.where(replaced, placed, cached.astype(jnp.float32)).astype(jnp.bfloat16)
    key_value = blended.reshape(spans * span_len, kv_heads, 2, HEAD).astype(jnp.float32)
    query_rows = request_queries.reshape(spans * per_span, kv_heads, head_group, HEAD).astype(jnp.float32)
    scores = jnp.einsum('qhgd,khd->hgqk', query_rows, key_value[:, :, 0]) * (1.0 / math.sqrt(HEAD))
    query_span = jnp.arange(spans * per_span) // per_span
    key_span = jnp.arange(spans * span_len) // span_len
    key_place = jnp.arange(spans * span_len) % span_len
    query_place = recompute_pos.reshape(-1)
    query_rank = jnp.repeat(span_rank, per_span)
    key_rank = jnp.repeat(span_rank, span_len)
    earlier = key_rank[None, :] < query_rank[:, None]
    causal = (key_span[None, :] == query_span[:, None]) & (key_place[None, :] <= query_place[:, None])
    allowed = earlier | causal
    scores = jnp.where(allowed[None, None], scores, -1e+30)
    peak = lax.optimization_barrier(jnp.max(scores, axis=-1, keepdims=True))
    raised = jnp.exp(scores - peak)
    weights = (raised / lax.optimization_barrier(jnp.sum(raised, axis=-1, keepdims=True))).astype(jnp.bfloat16)
    mixed = jnp.einsum('hgqk,khd->qhgd', weights.astype(jnp.float32), key_value[:, :, 1])
    mixed = mixed.reshape(spans * per_span, -1) * row_used.reshape(-1, 1).astype(jnp.float32)
    return mixed.astype(jnp.bfloat16)

def reference(hidden, kv_weight, pages, queries, page_owner, page_slot, span_order, positions, counts):
    rows_request = SPANS * RB
    hidden_request = hidden.reshape(REQUESTS, rows_request, D)
    query_request = queries.reshape(REQUESTS, rows_request, QH * HEAD)
    page_index = (page_owner * SLOTS + page_slot).astype(jnp.int32)

    def one_request(inputs):
        hidden_rows, query_rows, index_row, rank_row, position_rows, count_row = inputs
        row_used = jnp.arange(RB)[None, :] < count_row[:, None]
        fresh_rows = jnp.dot(hidden_rows, kv_weight, preferred_element_type=jnp.float32)
        fresh_rows = (fresh_rows * row_used.reshape(-1, 1).astype(jnp.float32)).astype(jnp.bfloat16)
        cached = jnp.take(pages, index_row, axis=0)
        mixed = blend_attend(query_rows, fresh_rows, cached, rank_row, position_rows, row_used)
        return (mixed, fresh_rows)
    attended, new_kv = lax.map(one_request, (hidden_request, query_request, page_index, span_order, positions, counts))
    return (attended.reshape(ROWS, QH * HEAD), new_kv.reshape(ROWS, KVH * 2 * HEAD))
```

```python
import functools

import jax
import jax.numpy as jnp
from jax import lax
from jax.experimental import pallas as pl
from jax.experimental.pallas import tpu as pltpu
from jax.sharding import PartitionSpec as P

HEAD = 128
MESH_ID = pl.DeviceIdType.MESH
ROW_TILE = 256
VMEM_BYTES = 60 * 1024 * 1024


def exchange_kernel(
    line, tensors, hid_ref, w_ref, out_ref, used_ref, kv_ref, arr_ref,
    wbuf, own, sendbuf, recvbuf,
    loc_sem, up_sem, dn_sem, x_sem, wrecv, psend, precv, rsend, rrecv,
):
    me = lax.axis_index("store")
    tm = lax.axis_index("tensor")
    n = 2 * line
    a, b = me // 2, me % 2
    width = w_ref.shape[1]
    per_owner = (n * width) // (tensors * width)

    barrier = pltpu.get_barrier_semaphore()
    for j in range(1, n):
        pl.semaphore_signal(
            barrier, inc=1, device_id=((me + j) % n, tm), device_id_type=MESH_ID
        )
    for j in range(1, tensors):
        pl.semaphore_signal(
            barrier, inc=1, device_id=(me, (tm + j) % tensors), device_id_type=MESH_ID
        )
    own_w = pltpu.make_async_copy(w_ref, wbuf.at[me], loc_sem.at[0])
    own_w.start()
    own_pages = pltpu.make_async_copy(out_ref.at[me], arr_ref.at[me], loc_sem.at[1])
    own_pages.start()
    own_w.wait()
    pl.semaphore_wait(barrier, n - 1 + tensors - 1)

    def w_copy(slot, sem, dest):
        return pltpu.make_async_remote_copy(
            src_ref=wbuf.at[slot], dst_ref=wbuf.at[slot], send_sem=sem.at[slot],
            recv_sem=wrecv.at[slot], device_id=(dest, tm), device_id_type=MESH_ID,
        )

    def up(slot):
        return w_copy(slot, up_sem, jnp.minimum(me + 2, n - 2 + b))

    def down(slot):
        return w_copy(slot, dn_sem, jnp.maximum(me - 2, b))

    def across(slot):
        return w_copy(slot, x_sem, a * 2 + 1 - b)

    def got(slot):
        across(slot).wait_recv()

    def page_copy(dest):
        return pltpu.make_async_remote_copy(
            src_ref=out_ref.at[dest], dst_ref=arr_ref.at[me], send_sem=psend.at[dest],
            recv_sem=precv.at[me], device_id=(dest, tm), device_id_type=MESH_ID,
        )

    def page_wait(src):
        pltpu.make_async_remote_copy(
            src_ref=out_ref.at[src], dst_ref=arr_ref.at[src], send_sem=psend.at[src],
            recv_sem=precv.at[src], device_id=(src, tm), device_id_type=MESH_ID,
        ).wait_recv()

    def part_copy(slot):
        return pltpu.make_async_remote_copy(
            src_ref=sendbuf.at[slot], dst_ref=recvbuf.at[tm, slot % per_owner],
            send_sem=rsend.at[slot], recv_sem=rrecv.at[tm, slot % per_owner],
            device_id=(me, slot // per_owner), device_id_type=MESH_ID,
        )

    def compute(slot):
        mine = slot // per_owner == tm

        def tile(i, carry):
            rows = pl.ds(pl.multiple_of(i * ROW_TILE, ROW_TILE), ROW_TILE)
            part = jnp.dot(hid_ref[rows, :], wbuf[slot], preferred_element_type=jnp.float32)

            @pl.when(mine)
            def _():
                own[slot % per_owner, rows, :] = part

            @pl.when(jnp.logical_not(mine))
            def _():
                sendbuf[slot, rows, :] = part.astype(sendbuf.dtype)

            return carry

        lax.fori_loop(0, hid_ref.shape[0] // ROW_TILE, tile, 0)

        @pl.when(jnp.logical_not(mine))
        def _():
            part_copy(slot).start()

    @pl.when(a < line - 1)
    def _():
        up(me).start()

    @pl.when(a > 0)
    def _():
        down(me).start()

    across(me).start()
    compute(me)

    def hop(k, carry):
        low, high = a - k, a + k

        @pl.when(low >= 0)
        def _():
            slot = low * 2 + b
            got(slot)

            @pl.when(a < line - 1)
            def _():
                up(slot).start()

            across(slot).start()

        @pl.when(high < line)
        def _():
            slot = high * 2 + b
            got(slot)

            @pl.when(a > 0)
            def _():
                down(slot).start()

            across(slot).start()

        @pl.when(k == 1)
        def _():
            def same(i, c):
                page_copy(((a + i) % line) * 2 + b).start()
                return c

            lax.fori_loop(1, line, same, 0)

        @pl.when(k == line - 1)
        def _():
            def other(i, c):
                page_copy(((a + i) % line) * 2 + 1 - b).start()
                return c

            lax.fori_loop(0, line, other, 0)

        for place in (low, high):
            @pl.when((place >= 0) & (place < line))
            def _(place=place):
                compute(place * 2 + b)

        return carry

    lax.fori_loop(1, line, hop, 0)

    def cross(k, carry):
        for place in (a - k, a + k):
            @pl.when((place >= 0) & (place < line))
            def _(place=place):
                slot = place * 2 + 1 - b
                got(slot)
                compute(slot)

        return carry

    slot0 = a * 2 + 1 - b
    got(slot0)
    compute(slot0)
    lax.fori_loop(1, line, cross, 0)

    def collect(j, carry):
        src = (tm + j) % tensors
        for q in range(per_owner):
            pltpu.make_async_remote_copy(
                src_ref=sendbuf.at[q], dst_ref=recvbuf.at[src, q], send_sem=rsend.at[q],
                recv_sem=rrecv.at[src, q], device_id=(me, src), device_id_type=MESH_ID,
            ).wait_recv()
        return carry

    lax.fori_loop(1, tensors, collect, 0)

    def finish(i, carry):
        rows = pl.ds(pl.multiple_of(i * ROW_TILE, ROW_TILE), ROW_TILE)
        for q in range(per_owner):
            total = own[q, rows, :]
            for j in range(1, tensors):
                total += recvbuf[(tm + j) % tensors, q, rows, :].astype(jnp.float32)
            kv_ref[rows, q * width : (q + 1) * width] = (total * used_ref[rows, :]).astype(
                kv_ref.dtype
            )
        return carry

    lax.fori_loop(0, hid_ref.shape[0] // ROW_TILE, finish, 0)

    def drain(slot, carry):
        @pl.when(slot // per_owner != tm)
        def _():
            part_copy(slot).wait_send()

        @pl.when(slot % 2 == b)
        def _():
            across(slot).wait_send()

            @pl.when((slot // 2 <= a) & (a < line - 1))
            def _():
                up(slot).wait_send()

            @pl.when((slot // 2 >= a) & (a > 0))
            def _():
                down(slot).wait_send()

        @pl.when(slot != me)
        def _():
            page_copy(slot).wait_send()
            page_wait(slot)

        return carry

    lax.fori_loop(0, n, drain, 0)
    own_pages.wait()


def exchange(hidden, kv_weight, outgoing, used, n, tensors):
    rows, depth = hidden.shape
    width = kv_weight.shape[1]
    per_owner = n // tensors
    dma = pltpu.SemaphoreType.DMA
    return pl.pallas_call(
        functools.partial(exchange_kernel, n // 2, tensors),
        out_shape=(
            jax.ShapeDtypeStruct((rows, per_owner * width), jnp.bfloat16),
            jax.ShapeDtypeStruct(outgoing.shape, outgoing.dtype),
        ),
        in_specs=[
            pl.BlockSpec(memory_space=pltpu.VMEM),
            pl.BlockSpec(memory_space=pl.ANY),
            pl.BlockSpec(memory_space=pl.ANY),
            pl.BlockSpec(memory_space=pltpu.VMEM),
        ],
        out_specs=(
            pl.BlockSpec(memory_space=pltpu.VMEM),
            pl.BlockSpec(memory_space=pl.ANY),
        ),
        scratch_shapes=[
            pltpu.VMEM((n, depth, width), jnp.bfloat16),
            pltpu.VMEM((per_owner, rows, width), jnp.float32),
            pltpu.VMEM((n, rows, width), jnp.bfloat16),
            pltpu.VMEM((tensors, per_owner, rows, width), jnp.bfloat16),
            dma((2,)), dma((n,)), dma((n,)), dma((n,)), dma((n,)),
            dma((n,)), dma((n,)), dma((n,)), dma((tensors, per_owner)),
        ],
        compiler_params=pltpu.CompilerParams(
            collective_id=0, has_side_effects=True, vmem_limit_bytes=VMEM_BYTES
        ),
        cost_estimate=pl.CostEstimate(
            flops=2 * rows * depth * n * width, bytes_accessed=4 * 10**7, transcendentals=0
        ),
    )(hidden, kv_weight, outgoing, used)


GROUP = 4


def attend_kernel(
    reqs, spans, per_span, span_len, heads, fold,
    page_sref, span_sref, q_ref, kv_ref, pos_col, used_col, pos_row, arr_ref, out_ref,
    page, keys, qbuf, sbuf, lim, page_sem,
):
    def fetch(i):
        return pltpu.make_async_copy(arr_ref.at[page_sref[i]], page.at[i], page_sem.at[i])

    def start(i, c):
        fetch(i).start()
        return c

    lax.fori_loop(0, reqs * spans, start, 0)

    def blend(i, c):
        fetch(i).wait()
        span = span_sref[i]
        marks = pos_row[pl.ds(span, 1), :]
        hit = lax.broadcasted_iota(jnp.int32, (span_len, per_span), 0) == marks
        fresh = kv_ref[pl.ds(pl.multiple_of(span * per_span, per_span), per_span), :]
        placed = jnp.dot(
            hit.astype(jnp.float32).astype(jnp.bfloat16), fresh,
            preferred_element_type=jnp.float32,
        )
        replaced = jnp.max(hit.astype(jnp.float32), axis=1, keepdims=True) > 0.5
        mixed = jnp.where(replaced, placed, page[i].astype(jnp.float32))
        keys[pl.ds(pl.multiple_of(i * span_len, span_len), span_len), :] = mixed.astype(
            jnp.bfloat16
        )
        return c

    lax.fori_loop(0, reqs * spans, blend, 0)
    scale = HEAD ** (-0.5)
    block = fold * per_span

    def one(i, carry):
        r = i // (spans // GROUP)
        for g_static in range(spans // GROUP):
            @pl.when(i % (spans // GROUP) == g_static)
            def _(g=g_static):
                length = (g + 1) * GROUP * span_len
                free = g * GROUP * span_len
                base = pl.multiple_of(r * spans * span_len, span_len)
                for h in range(heads):
                    for ii in range(GROUP):
                        span = span_sref[r * spans + g * GROUP + ii]
                        rows = pl.ds(pl.multiple_of(span * per_span, per_span), per_span)
                        limit = pos_col[rows, :] + ii * span_len
                        for m in range(fold):
                            col = (h * fold + m) * HEAD
                            at = ii * block + m * per_span
                            qbuf[at : at + per_span, :] = q_ref[rows, col : col + HEAD]
                            if h == 0:
                                lim[at : at + per_span, :] = limit
                    key = keys[pl.ds(base, length), 2 * h * HEAD : (2 * h + 1) * HEAD]
                    val = keys[pl.ds(base, length), (2 * h + 1) * HEAD : (2 * h + 2) * HEAD]
                    sbuf[:, :length] = lax.dot_general(
                        qbuf[...], key, (((1,), (1,)), ((), ())),
                        preferred_element_type=jnp.float32,
                    )
                    for ii in range(GROUP):
                        sl = slice(ii * block, (ii + 1) * block)
                        tail = sbuf[sl, free:length]
                        place = lax.broadcasted_iota(jnp.int32, tail.shape, 1)
                        tail = jnp.where(place <= lim[sl, :], tail, -1e30)
                        if g:
                            score = jnp.concatenate([sbuf[sl, :free], tail], axis=1)
                        else:
                            score = tail
                        peak = jnp.max(score, axis=1, keepdims=True)
                        raised = jnp.exp((score - peak) * scale)
                        total = jnp.sum(raised, axis=1, keepdims=True)
                        mixed = jnp.dot(
                            raised.astype(jnp.bfloat16), val, preferred_element_type=jnp.float32
                        ) / total
                        span = span_sref[r * spans + g * GROUP + ii]
                        rows = pl.ds(pl.multiple_of(span * per_span, per_span), per_span)
                        used = used_col[rows, :]
                        for m in range(fold):
                            col = (h * fold + m) * HEAD
                            out_ref[rows, col : col + HEAD] = (
                                mixed[m * per_span : (m + 1) * per_span, :] * used
                            ).astype(out_ref.dtype)
        return carry

    lax.fori_loop(0, reqs * (spans // GROUP), one, 0)


def attend(page_at, span_at, queries, new_kv, pos_col, used_col, pos_row, arrived, shape):
    reqs, spans, per_span, span_len = shape
    heads = new_kv.shape[1] // (2 * HEAD)
    fold = queries.shape[1] // (heads * HEAD)
    vm = pl.BlockSpec(memory_space=pltpu.VMEM)
    sm = pl.BlockSpec(memory_space=pltpu.SMEM)
    total = reqs * spans
    return pl.pallas_call(
        functools.partial(attend_kernel, reqs, spans, per_span, span_len, heads, fold),
        out_shape=jax.ShapeDtypeStruct(queries.shape, queries.dtype),
        in_specs=[sm, sm, vm, vm, vm, vm, vm, pl.BlockSpec(memory_space=pl.ANY)],
        out_specs=vm,
        scratch_shapes=[
            pltpu.VMEM((total, span_len, new_kv.shape[1]), jnp.bfloat16),
            pltpu.VMEM((total * span_len, new_kv.shape[1]), jnp.bfloat16),
            pltpu.VMEM((GROUP * fold * per_span, HEAD), jnp.bfloat16),
            pltpu.VMEM((GROUP * fold * per_span, spans * span_len), jnp.float32),
            pltpu.VMEM((GROUP * fold * per_span, 1), jnp.int32),
            pltpu.SemaphoreType.DMA((total,)),
        ],
        compiler_params=pltpu.CompilerParams(vmem_limit_bytes=VMEM_BYTES),
    )(page_at, span_at, queries, new_kv, pos_col, used_col, pos_row, arrived)


def body(hidden, kv_weight, pages, queries, page_owner, page_slot, span_order, positions, counts):
    store_count = lax.axis_size("store")
    tensors = lax.axis_size("tensor")
    store_index = lax.axis_index("store")
    req_local, spans = span_order.shape
    per_span = positions.shape[2]
    entries = req_local * spans
    slot_depth = max(2, 2 * entries // store_count)
    span_len = pages.shape[1]
    kv_width = pages.shape[2]
    row_used = jnp.arange(per_span)[None, None, :] < counts[:, :, None]
    used_col = row_used.reshape(-1, 1).astype(jnp.float32)
    owners = page_owner.reshape(store_count, entries)
    slot_table = page_slot.reshape(store_count, entries)
    before = jnp.arange(entries)[None, :] < jnp.arange(entries)[:, None]
    same_owner = owners[:, :, None] == owners[:, None, :]
    owner_rank = jnp.sum(same_owner & before[None], axis=2)
    picked = (owners == store_index)[:, :, None] & (
        owner_rank[:, :, None] == jnp.arange(slot_depth)[None, None, :]
    )
    source_slot = jnp.sum(picked * slot_table[:, :, None], axis=1)
    outgoing = jnp.take(pages, source_slot.reshape(-1), axis=0, mode="clip")
    outgoing = outgoing.reshape(store_count, slot_depth, span_len, kv_width)
    if kv_weight.shape[1] % 128 == 0 and store_count % tensors == 0:
        new_kv, arrived = exchange(hidden, kv_weight, outgoing, used_col, store_count, tensors)
    else:
        partial_kv = jnp.dot(
            hidden,
            lax.all_gather(kv_weight, "store", axis=1, tiled=True),
            preferred_element_type=jnp.float32,
        )
        own_kv = lax.psum_scatter(partial_kv, "tensor", scatter_dimension=1, tiled=True)
        new_kv = (own_kv * used_col).astype(jnp.bfloat16)
        arrived = lax.all_to_all(outgoing, "store", split_axis=0, concat_axis=0, tiled=True)
    my_owner = lax.dynamic_index_in_dim(owners, store_index, 0, keepdims=False)
    my_rank = lax.dynamic_index_in_dim(owner_rank, store_index, 0, keepdims=False)
    flat_index = (my_owner * slot_depth + my_rank).reshape(req_local, spans)
    is_place = span_order[:, None, :] == jnp.arange(spans)[None, :, None]
    span_at = jnp.sum(is_place * jnp.arange(spans)[None, None, :], axis=2)
    page_at = jnp.sum(is_place * flat_index[:, None, :], axis=2)
    span_at = (span_at + jnp.arange(req_local)[:, None] * spans).reshape(-1)
    attended = attend(
        page_at.reshape(-1).astype(jnp.int32), span_at.astype(jnp.int32), queries, new_kv,
        positions.reshape(-1, 1), used_col,
        jnp.where(row_used, positions, -1).reshape(entries, per_span),
        arrived.reshape(store_count * slot_depth, span_len, kv_width),
        (req_local, spans, per_span, span_len),
    )
    return (attended, new_kv)


def solution(mesh):
    placed = (
        P("store", "tensor"),
        P("tensor", "store"),
        P("store", None, "tensor"),
        P("store", "tensor"),
        P(),
        P(),
        P("store", None),
        P("store", None, None),
        P("store", None),
    )
    return jax.shard_map(
        body,
        mesh=mesh,
        in_specs=placed,
        out_specs=(P("store", "tensor"), P("store", "tensor")),
        check_vma=False,
    )
```

```python
import functools

import jax
import jax.numpy as jnp
from jax import lax
from jax.experimental import pallas as pl
from jax.experimental.pallas import tpu as pltpu
from jax.sharding import PartitionSpec as P

HEAD = 128
MESH_ID = pl.DeviceIdType.MESH
ROW_TILE = 256
VMEM_BYTES = 60 * 1024 * 1024


def exchange_kernel(
    line, tensors, pick_ref, hid_ref, w_ref, page_ref, used_ref, kv_ref, arr_ref,
    out_ref, wbuf, own, sendbuf, recvbuf,
    loc_sem, up_sem, dn_sem, x_sem, wrecv, psend, precv, rsend, rrecv,
):
    me = lax.axis_index("store")
    tm = lax.axis_index("tensor")
    n = 2 * line
    a, b = me // 2, me % 2
    width = w_ref.shape[1]
    per_owner = (n * width) // (tensors * width)

    barrier = pltpu.get_barrier_semaphore()
    for j in range(1, n):
        pl.semaphore_signal(
            barrier, inc=1, device_id=((me + j) % n, tm), device_id_type=MESH_ID
        )
    for j in range(1, tensors):
        pl.semaphore_signal(
            barrier, inc=1, device_id=(me, (tm + j) % tensors), device_id_type=MESH_ID
        )
    own_w = pltpu.make_async_copy(w_ref, wbuf.at[me], loc_sem.at[0])
    own_w.start()
    own_w.wait()
    pl.semaphore_wait(barrier, n - 1 + tensors - 1)

    def w_copy(slot, sem, dest):
        return pltpu.make_async_remote_copy(
            src_ref=wbuf.at[slot], dst_ref=wbuf.at[slot], send_sem=sem.at[slot],
            recv_sem=wrecv.at[slot], device_id=(dest, tm), device_id_type=MESH_ID,
        )

    def up(slot):
        return w_copy(slot, up_sem, jnp.minimum(me + 2, n - 2 + b))

    def down(slot):
        return w_copy(slot, dn_sem, jnp.maximum(me - 2, b))

    def across(slot):
        return w_copy(slot, x_sem, a * 2 + 1 - b)

    def got(slot):
        across(slot).wait_recv()

    def page_copy(dest):
        return pltpu.make_async_remote_copy(
            src_ref=out_ref.at[dest], dst_ref=arr_ref.at[me], send_sem=psend.at[dest],
            recv_sem=precv.at[me], device_id=(dest, tm), device_id_type=MESH_ID,
        )

    def page_wait(src):
        pltpu.make_async_remote_copy(
            src_ref=out_ref.at[src], dst_ref=arr_ref.at[src], send_sem=psend.at[src],
            recv_sem=precv.at[src], device_id=(src, tm), device_id_type=MESH_ID,
        ).wait_recv()

    def part_copy(slot):
        return pltpu.make_async_remote_copy(
            src_ref=sendbuf.at[slot], dst_ref=recvbuf.at[tm, slot % per_owner],
            send_sem=rsend.at[slot], recv_sem=rrecv.at[tm, slot % per_owner],
            device_id=(me, slot // per_owner), device_id_type=MESH_ID,
        )

    def compute(slot):
        mine = slot // per_owner == tm

        def tile(i, carry):
            rows = pl.ds(pl.multiple_of(i * ROW_TILE, ROW_TILE), ROW_TILE)
            part = jnp.dot(hid_ref[rows, :], wbuf[slot], preferred_element_type=jnp.float32)

            @pl.when(mine)
            def _():
                own[slot % per_owner, rows, :] = part

            @pl.when(jnp.logical_not(mine))
            def _():
                sendbuf[slot, rows, :] = part.astype(sendbuf.dtype)

            return carry

        lax.fori_loop(0, hid_ref.shape[0] // ROW_TILE, tile, 0)

        @pl.when(jnp.logical_not(mine))
        def _():
            part_copy(slot).start()

    @pl.when(a < line - 1)
    def _():
        up(me).start()

    @pl.when(a > 0)
    def _():
        down(me).start()

    across(me).start()
    depth = out_ref.shape[1]

    def choose(i, carry):
        out_ref[i // depth, i % depth] = page_ref[pick_ref[i]]
        return carry

    lax.fori_loop(0, n * depth, choose, 0)
    own_pages = pltpu.make_async_copy(out_ref.at[me], arr_ref.at[me], loc_sem.at[1])
    own_pages.start()
    compute(me)

    def hop(k, carry):
        low, high = a - k, a + k

        @pl.when(low >= 0)
        def _():
            slot = low * 2 + b
            got(slot)

            @pl.when(a < line - 1)
            def _():
                up(slot).start()

            across(slot).start()

        @pl.when(high < line)
        def _():
            slot = high * 2 + b
            got(slot)

            @pl.when(a > 0)
            def _():
                down(slot).start()

            across(slot).start()

        @pl.when(k == 2)
        def _():
            def launch(i, c):
                place = jnp.where(2 * a >= line, i, line - 1 - i)

                @pl.when(place != a)
                def _():
                    page_copy(place * 2 + b).start()

                page_copy(place * 2 + 1 - b).start()
                return c

            lax.fori_loop(0, line, launch, 0)

        for place in (low, high):
            @pl.when((place >= 0) & (place < line))
            def _(place=place):
                compute(place * 2 + b)

        return carry

    lax.fori_loop(1, line, hop, 0)

    def cross(k, carry):
        for place in (a - k, a + k):
            @pl.when((place >= 0) & (place < line))
            def _(place=place):
                slot = place * 2 + 1 - b
                got(slot)
                compute(slot)

        return carry

    slot0 = a * 2 + 1 - b
    got(slot0)
    compute(slot0)
    lax.fori_loop(1, line, cross, 0)

    def collect(j, carry):
        src = (tm + j) % tensors
        for q in range(per_owner):
            pltpu.make_async_remote_copy(
                src_ref=sendbuf.at[q], dst_ref=recvbuf.at[src, q], send_sem=rsend.at[q],
                recv_sem=rrecv.at[src, q], device_id=(me, src), device_id_type=MESH_ID,
            ).wait_recv()
        return carry

    lax.fori_loop(1, tensors, collect, 0)

    def finish(i, carry):
        rows = pl.ds(pl.multiple_of(i * ROW_TILE, ROW_TILE), ROW_TILE)
        for q in range(per_owner):
            total = own[q, rows, :]
            for j in range(1, tensors):
                total += recvbuf[(tm + j) % tensors, q, rows, :].astype(jnp.float32)
            kv_ref[rows, q * width : (q + 1) * width] = (total * used_ref[rows, :]).astype(
                kv_ref.dtype
            )
        return carry

    lax.fori_loop(0, hid_ref.shape[0] // ROW_TILE, finish, 0)

    def drain(slot, carry):
        @pl.when(slot // per_owner != tm)
        def _():
            part_copy(slot).wait_send()

        @pl.when(slot % 2 == b)
        def _():
            across(slot).wait_send()

            @pl.when((slot // 2 <= a) & (a < line - 1))
            def _():
                up(slot).wait_send()

            @pl.when((slot // 2 >= a) & (a > 0))
            def _():
                down(slot).wait_send()

        @pl.when(slot != me)
        def _():
            page_copy(slot).wait_send()
            page_wait(slot)

        return carry

    lax.fori_loop(0, n, drain, 0)
    own_pages.wait()


def exchange(picks, hidden, kv_weight, pages, depth_slots, used, n, tensors):
    rows, depth = hidden.shape
    width = kv_weight.shape[1]
    per_owner = n // tensors
    dma = pltpu.SemaphoreType.DMA
    return pl.pallas_call(
        functools.partial(exchange_kernel, n // 2, tensors),
        out_shape=(
            jax.ShapeDtypeStruct((rows, per_owner * width), jnp.bfloat16),
            jax.ShapeDtypeStruct((n, depth_slots) + pages.shape[1:], pages.dtype),
        ),
        in_specs=[
            pl.BlockSpec(memory_space=pltpu.SMEM),
            pl.BlockSpec(memory_space=pltpu.VMEM),
            pl.BlockSpec(memory_space=pl.ANY),
            pl.BlockSpec(memory_space=pltpu.VMEM),
            pl.BlockSpec(memory_space=pltpu.VMEM),
        ],
        out_specs=(
            pl.BlockSpec(memory_space=pltpu.VMEM),
            pl.BlockSpec(memory_space=pl.ANY),
        ),
        scratch_shapes=[
            pltpu.VMEM((n, depth_slots) + pages.shape[1:], pages.dtype),
            pltpu.VMEM((n, depth, width), jnp.bfloat16),
            pltpu.VMEM((per_owner, rows, width), jnp.float32),
            pltpu.VMEM((n, rows, width), jnp.bfloat16),
            pltpu.VMEM((tensors, per_owner, rows, width), jnp.bfloat16),
            dma((2,)), dma((n,)), dma((n,)), dma((n,)), dma((n,)),
            dma((n,)), dma((n,)), dma((n,)), dma((tensors, per_owner)),
        ],
        compiler_params=pltpu.CompilerParams(
            collective_id=0, has_side_effects=True, vmem_limit_bytes=VMEM_BYTES
        ),
        cost_estimate=pl.CostEstimate(
            flops=2 * rows * depth * n * width, bytes_accessed=4 * 10**7, transcendentals=0
        ),
    )(picks, hidden, kv_weight, pages, used)


GROUP = 4


def attend_kernel(
    reqs, spans, per_span, span_len, heads, fold,
    page_sref, span_sref, q_ref, kv_ref, pos_col, used_col, pos_row, arr_ref, out_ref,
    page, keys, qbuf, sbuf, lim, page_sem,
):
    def fetch(i):
        return pltpu.make_async_copy(arr_ref.at[page_sref[i]], page.at[i], page_sem.at[i])

    def start(i, c):
        fetch(i).start()
        return c

    lax.fori_loop(0, reqs * spans, start, 0)

    def blend(i, c):
        fetch(i).wait()
        span = span_sref[i]
        marks = pos_row[pl.ds(span, 1), :]
        hit = lax.broadcasted_iota(jnp.int32, (span_len, per_span), 0) == marks
        fresh = kv_ref[pl.ds(pl.multiple_of(span * per_span, per_span), per_span), :]
        placed = jnp.dot(
            hit.astype(jnp.float32).astype(jnp.bfloat16), fresh,
            preferred_element_type=jnp.float32,
        )
        replaced = jnp.max(hit.astype(jnp.float32), axis=1, keepdims=True) > 0.5
        mixed = jnp.where(replaced, placed, page[i].astype(jnp.float32))
        keys[pl.ds(pl.multiple_of(i * span_len, span_len), span_len), :] = mixed.astype(
            jnp.bfloat16
        )
        return c

    lax.fori_loop(0, reqs * spans, blend, 0)
    scale = HEAD ** (-0.5) * 1.4426950408889634
    block = fold * per_span

    def one(i, carry):
        r = i // (spans // GROUP)
        for g_static in range(spans // GROUP):
            @pl.when(i % (spans // GROUP) == g_static)
            def _(g=g_static):
                length = (g + 1) * GROUP * span_len
                free = g * GROUP * span_len
                base = pl.multiple_of(r * spans * span_len, span_len)
                for ii in range(GROUP):
                    span = span_sref[r * spans + g * GROUP + ii]
                    rows = pl.ds(pl.multiple_of(span * per_span, per_span), per_span)
                    limit = pos_col[rows, :]
                    for m in range(fold):
                        at = ii * block + m * per_span
                        lim[at : at + per_span, :] = limit
                        for h in range(heads):
                            col = (h * fold + m) * HEAD
                            qbuf[h, at : at + per_span, :] = q_ref[rows, col : col + HEAD]
                for h in range(heads):
                    key = keys[pl.ds(base, length), 2 * h * HEAD : (2 * h + 1) * HEAD]
                    sbuf[h, :, :length] = lax.dot_general(
                        qbuf[h], key, (((1,), (1,)), ((), ())),
                        preferred_element_type=jnp.float32,
                    )
                for h in range(heads):
                    for ii in range(GROUP):
                        sl = slice(ii * block, (ii + 1) * block)
                        open_to = free + ii * span_len
                        last = sbuf[h, sl, open_to : open_to + span_len]
                        place = lax.broadcasted_iota(jnp.int32, last.shape, 1)
                        last = jnp.where(place <= lim[sl, :], last, -1e30)
                        peak = jnp.max(last, axis=1, keepdims=True)
                        if open_to:
                            peak = jnp.maximum(
                                peak, jnp.max(sbuf[h, sl, :open_to], axis=1, keepdims=True)
                            )
                        peak = peak * scale
                        raised = jnp.exp2(last * scale - peak)
                        total = jnp.sum(raised, axis=1, keepdims=True)
                        vcol = slice((2 * h + 1) * HEAD, (2 * h + 2) * HEAD)
                        mixed = jnp.dot(
                            raised.astype(jnp.bfloat16),
                            keys[pl.ds(base + open_to, span_len), vcol],
                            preferred_element_type=jnp.float32,
                        )
                        if open_to:
                            raised = jnp.exp2(sbuf[h, sl, :open_to] * scale - peak)
                            total += jnp.sum(raised, axis=1, keepdims=True)
                            mixed += jnp.dot(
                                raised.astype(jnp.bfloat16),
                                keys[pl.ds(base, open_to), vcol],
                                preferred_element_type=jnp.float32,
                            )
                        mixed = mixed / total
                        span = span_sref[r * spans + g * GROUP + ii]
                        rows = pl.ds(pl.multiple_of(span * per_span, per_span), per_span)
                        used = used_col[rows, :]
                        for m in range(fold):
                            col = (h * fold + m) * HEAD
                            out_ref[rows, col : col + HEAD] = (
                                mixed[m * per_span : (m + 1) * per_span, :] * used
                            ).astype(out_ref.dtype)
        return carry

    lax.fori_loop(0, reqs * (spans // GROUP), one, 0)


def attend(page_at, span_at, queries, new_kv, pos_col, used_col, pos_row, arrived, shape):
    reqs, spans, per_span, span_len = shape
    heads = new_kv.shape[1] // (2 * HEAD)
    fold = queries.shape[1] // (heads * HEAD)
    vm = pl.BlockSpec(memory_space=pltpu.VMEM)
    sm = pl.BlockSpec(memory_space=pltpu.SMEM)
    total = reqs * spans
    return pl.pallas_call(
        functools.partial(attend_kernel, reqs, spans, per_span, span_len, heads, fold),
        out_shape=jax.ShapeDtypeStruct(queries.shape, queries.dtype),
        in_specs=[sm, sm, vm, vm, vm, vm, vm, pl.BlockSpec(memory_space=pl.ANY)],
        out_specs=vm,
        scratch_shapes=[
            pltpu.VMEM((total, span_len, new_kv.shape[1]), jnp.bfloat16),
            pltpu.VMEM((total * span_len, new_kv.shape[1]), jnp.bfloat16),
            pltpu.VMEM((heads, GROUP * fold * per_span, HEAD), jnp.bfloat16),
            pltpu.VMEM((heads, GROUP * fold * per_span, spans * span_len), jnp.float32),
            pltpu.VMEM((GROUP * fold * per_span, 1), jnp.int32),
            pltpu.SemaphoreType.DMA((total,)),
        ],
        compiler_params=pltpu.CompilerParams(vmem_limit_bytes=VMEM_BYTES),
    )(page_at, span_at, queries, new_kv, pos_col, used_col, pos_row, arrived)


def body(hidden, kv_weight, pages, queries, page_owner, page_slot, span_order, positions, counts):
    store_count = lax.axis_size("store")
    tensors = lax.axis_size("tensor")
    store_index = lax.axis_index("store")
    req_local, spans = span_order.shape
    per_span = positions.shape[2]
    entries = req_local * spans
    slot_depth = max(2, 2 * entries // store_count)
    span_len = pages.shape[1]
    kv_width = pages.shape[2]
    row_used = jnp.arange(per_span)[None, None, :] < counts[:, :, None]
    used_col = row_used.reshape(-1, 1).astype(jnp.float32)
    owners = page_owner.reshape(store_count, entries)
    slot_table = page_slot.reshape(store_count, entries)
    before = jnp.arange(entries)[None, :] < jnp.arange(entries)[:, None]
    same_owner = owners[:, :, None] == owners[:, None, :]
    owner_rank = jnp.sum(same_owner & before[None], axis=2)
    picked = (owners == store_index)[:, :, None] & (
        owner_rank[:, :, None] == jnp.arange(slot_depth)[None, None, :]
    )
    source_slot = jnp.sum(picked * slot_table[:, :, None], axis=1)
    picks = source_slot.reshape(-1).astype(jnp.int32)
    if kv_weight.shape[1] % 128 == 0 and store_count % tensors == 0 and store_count >= 6:
        new_kv, arrived = exchange(
            picks, hidden, kv_weight, pages, slot_depth, used_col, store_count, tensors
        )
    else:
        partial_kv = jnp.dot(
            hidden,
            lax.all_gather(kv_weight, "store", axis=1, tiled=True),
            preferred_element_type=jnp.float32,
        )
        own_kv = lax.psum_scatter(partial_kv, "tensor", scatter_dimension=1, tiled=True)
        new_kv = (own_kv * used_col).astype(jnp.bfloat16)
        outgoing = jnp.take(pages, picks, axis=0, mode="clip").reshape(
            store_count, slot_depth, span_len, kv_width
        )
        arrived = lax.all_to_all(outgoing, "store", split_axis=0, concat_axis=0, tiled=True)
    my_owner = lax.dynamic_index_in_dim(owners, store_index, 0, keepdims=False)
    my_rank = lax.dynamic_index_in_dim(owner_rank, store_index, 0, keepdims=False)
    flat_index = (my_owner * slot_depth + my_rank).reshape(req_local, spans)
    is_place = span_order[:, None, :] == jnp.arange(spans)[None, :, None]
    span_at = jnp.sum(is_place * jnp.arange(spans)[None, None, :], axis=2)
    page_at = jnp.sum(is_place * flat_index[:, None, :], axis=2)
    span_at = (span_at + jnp.arange(req_local)[:, None] * spans).reshape(-1)
    attended = attend(
        page_at.reshape(-1).astype(jnp.int32), span_at.astype(jnp.int32), queries, new_kv,
        positions.reshape(-1, 1), used_col,
        jnp.where(row_used, positions, -1).reshape(entries, per_span),
        arrived.reshape(store_count * slot_depth, span_len, kv_width),
        (req_local, spans, per_span, span_len),
    )
    return (attended, new_kv)


def solution(mesh):
    placed = (
        P("store", "tensor"),
        P("tensor", "store"),
        P("store", None, "tensor"),
        P("store", "tensor"),
        P(),
        P(),
        P("store", None),
        P("store", None, None),
        P("store", None),
    )
    return jax.shard_map(
        body,
        mesh=mesh,
        in_specs=placed,
        out_specs=(P("store", "tensor"), P("store", "tensor")),
        check_vma=False,
    )
```

```python
import functools

import jax
import jax.numpy as jnp
from jax import lax
from jax.experimental import pallas as pl
from jax.experimental.pallas import tpu as pltpu
from jax.sharding import PartitionSpec as P

HEAD = 128
MESH_ID = pl.DeviceIdType.MESH


def as_column(row):
    count = row.shape[1]
    eye = lax.broadcasted_iota(jnp.int32, (count, count), 0) == lax.broadcasted_iota(
        jnp.int32, (count, count), 1
    )
    return jnp.sum(jnp.where(eye, row, 0.0), axis=1, keepdims=True)


ROW_TILE = 256
VMEM_BYTES = 60 * 1024 * 1024


def exchange_kernel(
    line, tensors, pick_ref, hid_ref, w_ref, page_ref, used_ref, kv_ref, arr_ref,
    out_ref, wbuf, own, sendbuf, recvbuf,
    loc_sem, up_sem, dn_sem, x_sem, wrecv, psend, precv, rsend, rrecv,
):
    me = lax.axis_index("store")
    tm = lax.axis_index("tensor")
    n = 2 * line
    a, b = me // 2, me % 2
    width = w_ref.shape[1]
    per_owner = (n * width) // (tensors * width)

    barrier = pltpu.get_barrier_semaphore()
    for j in range(1, n):
        pl.semaphore_signal(
            barrier, inc=1, device_id=((me + j) % n, tm), device_id_type=MESH_ID
        )
    for j in range(1, tensors):
        pl.semaphore_signal(
            barrier, inc=1, device_id=(me, (tm + j) % tensors), device_id_type=MESH_ID
        )
    own_w = pltpu.make_async_copy(w_ref, wbuf.at[me], loc_sem.at[0])
    own_w.start()
    own_w.wait()
    pl.semaphore_wait(barrier, n - 1 + tensors - 1)

    def w_copy(slot, sem, dest):
        return pltpu.make_async_remote_copy(
            src_ref=wbuf.at[slot], dst_ref=wbuf.at[slot], send_sem=sem.at[slot],
            recv_sem=wrecv.at[slot], device_id=(dest, tm), device_id_type=MESH_ID,
        )

    def up(slot):
        return w_copy(slot, up_sem, jnp.minimum(me + 2, n - 2 + b))

    def down(slot):
        return w_copy(slot, dn_sem, jnp.maximum(me - 2, b))

    def across(slot):
        return w_copy(slot, x_sem, a * 2 + 1 - b)

    def got(slot):
        across(slot).wait_recv()

    def page_copy(dest):
        return pltpu.make_async_remote_copy(
            src_ref=out_ref.at[dest], dst_ref=arr_ref.at[me], send_sem=psend.at[dest],
            recv_sem=precv.at[me], device_id=(dest, tm), device_id_type=MESH_ID,
        )

    def page_wait(src):
        pltpu.make_async_remote_copy(
            src_ref=out_ref.at[src], dst_ref=arr_ref.at[src], send_sem=psend.at[src],
            recv_sem=precv.at[src], device_id=(src, tm), device_id_type=MESH_ID,
        ).wait_recv()

    def part_copy(slot):
        return pltpu.make_async_remote_copy(
            src_ref=sendbuf.at[slot], dst_ref=recvbuf.at[tm, slot % per_owner],
            send_sem=rsend.at[slot], recv_sem=rrecv.at[tm, slot % per_owner],
            device_id=(me, slot // per_owner), device_id_type=MESH_ID,
        )

    def compute(slot):
        mine = slot // per_owner == tm

        def tile(i, carry):
            rows = pl.ds(pl.multiple_of(i * ROW_TILE, ROW_TILE), ROW_TILE)
            part = jnp.dot(hid_ref[rows, :], wbuf[slot], preferred_element_type=jnp.float32)

            @pl.when(mine)
            def _():
                own[slot % per_owner, rows, :] = part

            @pl.when(jnp.logical_not(mine))
            def _():
                sendbuf[slot, rows, :] = part.astype(sendbuf.dtype)

            return carry

        lax.fori_loop(0, hid_ref.shape[0] // ROW_TILE, tile, 0)

        @pl.when(jnp.logical_not(mine))
        def _():
            part_copy(slot).start()

    @pl.when(a < line - 1)
    def _():
        up(me).start()

    @pl.when(a > 0)
    def _():
        down(me).start()

    across(me).start()
    depth = out_ref.shape[1]

    def choose(i, carry):
        out_ref[i // depth, i % depth] = page_ref[pick_ref[i]]
        return carry

    lax.fori_loop(0, n * depth, choose, 0)
    own_pages = pltpu.make_async_copy(out_ref.at[me], arr_ref.at[me], loc_sem.at[1])
    own_pages.start()
    compute(me)

    def hop(k, carry):
        low, high = a - k, a + k

        @pl.when(low >= 0)
        def _():
            slot = low * 2 + b
            got(slot)

            @pl.when(a < line - 1)
            def _():
                up(slot).start()

            across(slot).start()

        @pl.when(high < line)
        def _():
            slot = high * 2 + b
            got(slot)

            @pl.when(a > 0)
            def _():
                down(slot).start()

            across(slot).start()

        @pl.when(k == 2)
        def _():
            def launch(i, c):
                place = jnp.where(2 * a >= line, i, line - 1 - i)

                @pl.when(place != a)
                def _():
                    page_copy(place * 2 + b).start()

                page_copy(place * 2 + 1 - b).start()
                return c

            lax.fori_loop(0, line, launch, 0)

        for place in (low, high):
            @pl.when((place >= 0) & (place < line))
            def _(place=place):
                compute(place * 2 + b)

        return carry

    lax.fori_loop(1, line, hop, 0)

    def cross(k, carry):
        for place in (a - k, a + k):
            @pl.when((place >= 0) & (place < line))
            def _(place=place):
                slot = place * 2 + 1 - b
                got(slot)
                compute(slot)

        return carry

    slot0 = a * 2 + 1 - b
    got(slot0)
    compute(slot0)
    lax.fori_loop(1, line, cross, 0)

    def collect(j, carry):
        src = (tm + j) % tensors
        for q in range(per_owner):
            pltpu.make_async_remote_copy(
                src_ref=sendbuf.at[q], dst_ref=recvbuf.at[src, q], send_sem=rsend.at[q],
                recv_sem=rrecv.at[src, q], device_id=(me, src), device_id_type=MESH_ID,
            ).wait_recv()
        return carry

    lax.fori_loop(1, tensors, collect, 0)

    groups, per_group = used_ref.shape

    def finish(i, carry):
        rows = pl.ds(pl.multiple_of(i * per_group, per_group), per_group)
        keep = as_column(used_ref[pl.ds(i, 1), :])
        for q in range(per_owner):
            total = own[q, rows, :]
            for j in range(1, tensors):
                total += recvbuf[(tm + j) % tensors, q, rows, :].astype(jnp.float32)
            kv_ref[rows, q * width : (q + 1) * width] = (total * keep).astype(kv_ref.dtype)
        return carry

    lax.fori_loop(0, groups, finish, 0)

    def drain(slot, carry):
        @pl.when(slot // per_owner != tm)
        def _():
            part_copy(slot).wait_send()

        @pl.when(slot % 2 == b)
        def _():
            across(slot).wait_send()

            @pl.when((slot // 2 <= a) & (a < line - 1))
            def _():
                up(slot).wait_send()

            @pl.when((slot // 2 >= a) & (a > 0))
            def _():
                down(slot).wait_send()

        @pl.when(slot != me)
        def _():
            page_copy(slot).wait_send()
            page_wait(slot)

        return carry

    lax.fori_loop(0, n, drain, 0)
    own_pages.wait()


def exchange(picks, hidden, kv_weight, pages, depth_slots, used, n, tensors):
    rows, depth = hidden.shape
    width = kv_weight.shape[1]
    per_owner = n // tensors
    dma = pltpu.SemaphoreType.DMA
    return pl.pallas_call(
        functools.partial(exchange_kernel, n // 2, tensors),
        out_shape=(
            jax.ShapeDtypeStruct((rows, per_owner * width), jnp.bfloat16),
            jax.ShapeDtypeStruct((n, depth_slots) + pages.shape[1:], pages.dtype),
        ),
        in_specs=[
            pl.BlockSpec(memory_space=pltpu.SMEM),
            pl.BlockSpec(memory_space=pltpu.VMEM),
            pl.BlockSpec(memory_space=pl.ANY),
            pl.BlockSpec(memory_space=pltpu.VMEM),
            pl.BlockSpec(memory_space=pltpu.VMEM),
        ],
        out_specs=(
            pl.BlockSpec(memory_space=pltpu.VMEM),
            pl.BlockSpec(memory_space=pl.ANY),
        ),
        scratch_shapes=[
            pltpu.VMEM((n, depth_slots) + pages.shape[1:], pages.dtype),
            pltpu.VMEM((n, depth, width), jnp.bfloat16),
            pltpu.VMEM((per_owner, rows, width), jnp.float32),
            pltpu.VMEM((n, rows, width), jnp.bfloat16),
            pltpu.VMEM((tensors, per_owner, rows, width), jnp.bfloat16),
            dma((2,)), dma((n,)), dma((n,)), dma((n,)), dma((n,)),
            dma((n,)), dma((n,)), dma((n,)), dma((tensors, per_owner)),
        ],
        compiler_params=pltpu.CompilerParams(
            collective_id=0, has_side_effects=True, vmem_limit_bytes=VMEM_BYTES
        ),
        cost_estimate=pl.CostEstimate(
            flops=2 * rows * depth * n * width, bytes_accessed=4 * 10**7, transcendentals=0
        ),
    )(picks, hidden, kv_weight, pages, used)


GROUP = 4


def attend_kernel(
    reqs, spans, per_span, span_len, heads, fold,
    page_sref, span_sref, q_ref, kv_ref, pos_row, arr_ref, out_ref,
    page, keys, qbuf, sbuf, lim, page_sem,
):
    def fetch(i):
        return pltpu.make_async_copy(arr_ref.at[page_sref[i]], page.at[i], page_sem.at[i])

    def start(i, c):
        fetch(i).start()
        return c

    lax.fori_loop(0, reqs * spans, start, 0)

    def blend_one(i):
        fetch(i).wait()
        span = span_sref[i]
        marks = pos_row[pl.ds(span, 1), :]
        hit = lax.broadcasted_iota(jnp.int32, (span_len, per_span), 0) == marks
        hit = hit.astype(jnp.float32)
        fresh = kv_ref[pl.ds(pl.multiple_of(span * per_span, per_span), per_span), :]
        kept = 1.0 - jnp.max(hit, axis=1, keepdims=True)
        eye = lax.broadcasted_iota(jnp.int32, (span_len, span_len), 0) == (
            lax.broadcasted_iota(jnp.int32, (span_len, span_len), 1)
        )
        kept = jnp.where(eye, kept, 0.0)
        mixed = jnp.dot(
            hit.astype(jnp.bfloat16), fresh, preferred_element_type=jnp.float32
        ) + jnp.dot(kept.astype(jnp.bfloat16), page[i], preferred_element_type=jnp.float32)
        keys[pl.ds(pl.multiple_of(i * span_len, span_len), span_len), :] = mixed.astype(
            jnp.bfloat16
        )

    def blend(i, c):
        for step in range(GROUP):
            blend_one(i * GROUP + step)
        return c

    lax.fori_loop(0, reqs * spans // GROUP, blend, 0)
    scale = HEAD ** (-0.5) * 1.4426950408889634
    block = fold * per_span

    def one(i, carry):
        r = i // (spans // GROUP)
        for g_static in range(spans // GROUP):
            @pl.when(i % (spans // GROUP) == g_static)
            def _(g=g_static):
                length = (g + 1) * GROUP * span_len
                free = g * GROUP * span_len
                base = pl.multiple_of(r * spans * span_len, span_len)
                useds = []
                for ii in range(GROUP):
                    span = span_sref[r * spans + g * GROUP + ii]
                    rows = pl.ds(pl.multiple_of(span * per_span, per_span), per_span)
                    limit = as_column(pos_row[pl.ds(span, 1), :].astype(jnp.float32))
                    useds.append((limit >= 0.0).astype(jnp.float32))
                    limit = limit.astype(jnp.int32)
                    for m in range(fold):
                        at = ii * block + m * per_span
                        lim[at : at + per_span, :] = limit
                        for h in range(heads):
                            col = (h * fold + m) * HEAD
                            qbuf[h, at : at + per_span, :] = q_ref[rows, col : col + HEAD]
                for h in range(heads):
                    key = keys[pl.ds(base, length), 2 * h * HEAD : (2 * h + 1) * HEAD]
                    sbuf[h, :, :length] = lax.dot_general(
                        qbuf[h], key, (((1,), (1,)), ((), ())),
                        preferred_element_type=jnp.float32,
                    )
                for h in range(heads):
                    for ii in range(GROUP):
                        sl = slice(ii * block, (ii + 1) * block)
                        open_to = free + ii * span_len
                        last = sbuf[h, sl, open_to : open_to + span_len]
                        place = lax.broadcasted_iota(jnp.int32, last.shape, 1)
                        last = jnp.where(place <= lim[sl, :], last, -1e30)
                        peak = jnp.max(last, axis=1, keepdims=True)
                        if open_to:
                            peak = jnp.maximum(
                                peak, jnp.max(sbuf[h, sl, :open_to], axis=1, keepdims=True)
                            )
                        peak = peak * scale
                        raised = jnp.exp2(last * scale - peak)
                        total = jnp.sum(raised, axis=1, keepdims=True)
                        vcol = slice((2 * h + 1) * HEAD, (2 * h + 2) * HEAD)
                        mixed = jnp.dot(
                            raised.astype(jnp.bfloat16),
                            keys[pl.ds(base + open_to, span_len), vcol],
                            preferred_element_type=jnp.float32,
                        )
                        if open_to:
                            raised = jnp.exp2(sbuf[h, sl, :open_to] * scale - peak)
                            total += jnp.sum(raised, axis=1, keepdims=True)
                            mixed += jnp.dot(
                                raised.astype(jnp.bfloat16),
                                keys[pl.ds(base, open_to), vcol],
                                preferred_element_type=jnp.float32,
                            )
                        mixed = mixed / total
                        span = span_sref[r * spans + g * GROUP + ii]
                        rows = pl.ds(pl.multiple_of(span * per_span, per_span), per_span)
                        used = useds[ii]
                        for m in range(fold):
                            col = (h * fold + m) * HEAD
                            out_ref[rows, col : col + HEAD] = (
                                mixed[m * per_span : (m + 1) * per_span, :] * used
                            ).astype(out_ref.dtype)
        return carry

    lax.fori_loop(0, reqs * (spans // GROUP), one, 0)


def attend(page_at, span_at, queries, new_kv, pos_row, arrived, shape):
    reqs, spans, per_span, span_len = shape
    heads = new_kv.shape[1] // (2 * HEAD)
    fold = queries.shape[1] // (heads * HEAD)
    vm = pl.BlockSpec(memory_space=pltpu.VMEM)
    sm = pl.BlockSpec(memory_space=pltpu.SMEM)
    total = reqs * spans
    return pl.pallas_call(
        functools.partial(attend_kernel, reqs, spans, per_span, span_len, heads, fold),
        out_shape=jax.ShapeDtypeStruct(queries.shape, queries.dtype),
        in_specs=[sm, sm, vm, vm, vm, pl.BlockSpec(memory_space=pl.ANY)],
        out_specs=vm,
        scratch_shapes=[
            pltpu.VMEM((total, span_len, new_kv.shape[1]), jnp.bfloat16),
            pltpu.VMEM((total * span_len, new_kv.shape[1]), jnp.bfloat16),
            pltpu.VMEM((heads, GROUP * fold * per_span, HEAD), jnp.bfloat16),
            pltpu.VMEM((heads, GROUP * fold * per_span, spans * span_len), jnp.float32),
            pltpu.VMEM((GROUP * fold * per_span, 1), jnp.int32),
            pltpu.SemaphoreType.DMA((total,)),
        ],
        compiler_params=pltpu.CompilerParams(vmem_limit_bytes=VMEM_BYTES),
    )(page_at, span_at, queries, new_kv, pos_row, arrived)


def body(hidden, kv_weight, pages, queries, page_owner, page_slot, span_order, positions, counts):
    store_count = lax.axis_size("store")
    tensors = lax.axis_size("tensor")
    store_index = lax.axis_index("store")
    req_local, spans = span_order.shape
    per_span = positions.shape[2]
    entries = req_local * spans
    slot_depth = max(2, 2 * entries // store_count)
    span_len = pages.shape[1]
    kv_width = pages.shape[2]
    row_used = jnp.arange(per_span)[None, None, :] < counts[:, :, None]
    used_row = row_used.reshape(entries, per_span).astype(jnp.float32)
    owners = page_owner.reshape(store_count, entries)
    slot_table = page_slot.reshape(store_count, entries)
    before = jnp.arange(entries)[None, :] < jnp.arange(entries)[:, None]
    same_owner = owners[:, :, None] == owners[:, None, :]
    owner_rank = jnp.sum(same_owner & before[None], axis=2)
    picked = (owners == store_index)[:, :, None] & (
        owner_rank[:, :, None] == jnp.arange(slot_depth)[None, None, :]
    )
    source_slot = jnp.sum(picked * slot_table[:, :, None], axis=1)
    picks = source_slot.reshape(-1).astype(jnp.int32)
    if kv_weight.shape[1] % 128 == 0 and store_count % tensors == 0 and store_count >= 6:
        new_kv, arrived = exchange(
            picks, hidden, kv_weight, pages, slot_depth, used_row, store_count, tensors
        )
    else:
        partial_kv = jnp.dot(
            hidden,
            lax.all_gather(kv_weight, "store", axis=1, tiled=True),
            preferred_element_type=jnp.float32,
        )
        own_kv = lax.psum_scatter(partial_kv, "tensor", scatter_dimension=1, tiled=True)
        new_kv = (own_kv * used_row.reshape(-1, 1)).astype(jnp.bfloat16)
        outgoing = jnp.take(pages, picks, axis=0, mode="clip").reshape(
            store_count, slot_depth, span_len, kv_width
        )
        arrived = lax.all_to_all(outgoing, "store", split_axis=0, concat_axis=0, tiled=True)
    my_owner = lax.dynamic_index_in_dim(owners, store_index, 0, keepdims=False)
    my_rank = lax.dynamic_index_in_dim(owner_rank, store_index, 0, keepdims=False)
    flat_index = (my_owner * slot_depth + my_rank).reshape(req_local, spans)
    is_place = span_order[:, None, :] == jnp.arange(spans)[None, :, None]
    span_at = jnp.sum(is_place * jnp.arange(spans)[None, None, :], axis=2)
    page_at = jnp.sum(is_place * flat_index[:, None, :], axis=2)
    span_at = (span_at + jnp.arange(req_local)[:, None] * spans).reshape(-1)
    attended = attend(
        page_at.reshape(-1).astype(jnp.int32), span_at.astype(jnp.int32), queries, new_kv,
        jnp.where(row_used, positions, -1).reshape(entries, per_span),
        arrived.reshape(store_count * slot_depth, span_len, kv_width),
        (req_local, spans, per_span, span_len),
    )
    return (attended, new_kv)


def solution(mesh):
    placed = (
        P("store", "tensor"),
        P("tensor", "store"),
        P("store", None, "tensor"),
        P("store", "tensor"),
        P(),
        P(),
        P("store", None),
        P("store", None, None),
        P("store", None),
    )
    return jax.shard_map(
        body,
        mesh=mesh,
        in_specs=placed,
        out_specs=(P("store", "tensor"), P("store", "tensor")),
        check_vma=False,
    )
```
